32 devices in a mesh: tm: 8 (over z, x), sta: 4 (over y, core).
Axes of the slice: x: 2, y: 2, z: 4, core: 2. Of those that a mesh axis runs over, the one named last changes fastest.
Arguments:
- voltages: bfloat16 [2, 4, 64, 262144], P(None, None, 'sta', 'tm'), may hold values from -6 to 6
- sample_delay: int32 [64, 8], P('sta', 'tm'), may hold values from 0 to 8192, as said below
- frac_index: int32 [64, 8], P('sta', 'tm'), may hold values from 0 to 63
- phase_index: int32 [4, 64, 8], P(None, 'sta', 'tm'), may hold values from 0 to 1023
- fringe_rate: float32 [4, 64], P(None, 'sta'), may hold values from -3 to 3
Outputs:
- visibilities: float32 [4, 16384, 64, 128], P(None, ('tm', 'sta'))
The draws below stay inside these ranges and needn't reach their ends.
Inputs may be any that keep to these rules, and one draw needn't show every extreme that they name: `sample_delay`: the largest delay, 8192, occurs in every draw.
All inputs are finite; a program needn't handle non-finite values.
Results may differ from the reference program's by a relative error of at most 0.0089.
Values may be sent and summed in bfloat16 or wider, within the bound.
A program may use at most 256 MiB of HBM per device.

```python
import math
import jax
import jax.numpy as jnp
from jax import lax

STATIONS = 64
SUBBANDS = 4
CHANNELS = 16384
RADIX_A = 128
RADIX_B = 128
FRAMES = 2
TAPS = 32
NFRAC = 64
NPHASE = 1024
MAXD = 8192
SLICES = 8
SAMPLES = 262144


def draw_sample_delay(key, part):
    key_values = jax.random.fold_in(key, 11)
    key_station = jax.random.fold_in(key, 12)
    key_slice = jax.random.fold_in(key, 13)
    delays = jax.random.randint(key_values, (STATIONS, SLICES), 0, MAXD + 1)
    station_at = jax.random.randint(key_station, (), 0, STATIONS)
    slice_at = jax.random.randint(key_slice, (), 0, SLICES)
    return delays.at[station_at, slice_at].set(MAXD).astype(jnp.int32)


def touch_ends(entries, stream_key, smallest, largest):
    longest = entries.shape.index(max(entries.shape))
    spots = []
    for shift in (0, 1):
        where = [jax.random.randint(jax.random.fold_in(stream_key, axis), (), 0, length) for axis, length in enumerate(entries.shape)]
        where[longest] = (where[longest] + shift) % entries.shape[longest]
        spots.append(tuple(where))
    return entries.at[spots[0]].set(smallest).at[spots[1]].set(largest)


def level_of(own_key, dims, shards, least, high):
    def one(dim, shards_of):
        steps = jax.random.uniform(jax.random.fold_in(jax.random.fold_in(own_key, 6), dim), (shards_of,), jnp.float32, least / len(shards), high / len(shards))
        return jnp.repeat(jnp.exp(steps), dims[dim] // shards_of).reshape((-1,) + (1,) * (len(dims) - dim - 1))

    gain = one(*shards[0])
    for cut in shards[1:]:
        gain = gain * one(*cut)
    return gain


def bell_draw(rng, shape, spread, most, shards=(), held_as=jnp.bfloat16):
    values = spread * jax.random.normal(rng, shape, jnp.float32)
    if shards:
        values = values * level_of(rng, shape, shards, -0.22, 0.18)
    return jnp.clip(values, -most, most).astype(held_as)


def setup_inputs(seed: int = 0) -> dict:
    key_of = jax.random.split(jax.random.key(seed), 6)
    voltages = bell_draw(key_of[0], (2, SUBBANDS, STATIONS, SAMPLES), 1.0, 6.0, ((2, 4), (3, 8)))
    sample_delay = draw_sample_delay(jax.random.fold_in(key_of[5], 71), 0)
    frac_index = touch_ends(jax.random.randint(key_of[2], (STATIONS, SLICES), 0, NFRAC), jax.random.fold_in(key_of[2], 1), 0, NFRAC - 1).astype(jnp.int32)
    phase_index = touch_ends(jax.random.randint(key_of[3], (SUBBANDS, STATIONS, SLICES), 0, NPHASE), jax.random.fold_in(key_of[3], 1), 0, NPHASE - 1).astype(jnp.int32)
    fringe_rate = jnp.clip(jax.random.uniform(key_of[4], (SUBBANDS, STATIONS), jnp.float32, -3.0, 3.0) * level_of(key_of[4], (SUBBANDS, STATIONS), ((1, 4),), -0.4, 0.0), -3.0, 3.0)
    return {"voltages": voltages, "sample_delay": sample_delay, "frac_index": frac_index, "phase_index": phase_index, "fringe_rate": fringe_rate}


def toeplitz_of(fraction_index):
    inputs_at = jnp.arange(256, dtype=jnp.int32)
    outputs_at = jnp.arange(128, dtype=jnp.int32)
    distance = inputs_at[:, None] - outputs_at[None, :]
    inside = (distance >= 0) & (distance < TAPS)
    fraction = fraction_index.astype(jnp.float32) / NFRAC
    offset = distance.astype(jnp.float32)
    centre = offset[None, :, :] - (TAPS // 2 - 1) - fraction[:, None, None]
    window_taper = 0.5 - 0.5 * jnp.cos(2.0 * jnp.pi * (offset + 0.5) / TAPS)
    values = jnp.sinc(centre) * window_taper[None, :, :]
    return jnp.where(inside[None, :, :], values, 0.0).astype(jnp.bfloat16)

def filter_rows(source, starts, kernel, sample_count):
    slicer = jax.vmap(lambda series, start_at: lax.dynamic_slice_in_dim(series, start_at, sample_count + 128, axis=1), in_axes=(1, 0), out_axes=1)
    pieces = slicer(source, starts)
    row_count = pieces.shape[1]
    blocks = sample_count // 128
    head_rows = pieces[:, :, :sample_count].reshape(2, row_count, blocks, 128)
    tail_rows = pieces[:, :, 128:].reshape(2, row_count, blocks, 128)
    windows = jnp.concatenate([head_rows, tail_rows], axis=-1)
    filtered = jnp.einsum('crnp,rpv->crnv', windows.astype(jnp.float32), kernel.astype(jnp.float32))
    return filtered.reshape(2, row_count, sample_count)

def rotate_rows(filtered, phase_rows, rate_rows, first_at, slice_length):
    sample_count = filtered.shape[-1]
    position = (jnp.arange(sample_count, dtype=jnp.int32) + first_at).astype(jnp.float32) / slice_length
    cycles = phase_rows.astype(jnp.float32)[:, None] / NPHASE + rate_rows[:, None] * position[None, :]
    phase_angle = 2.0 * jnp.pi * cycles
    cosine = jnp.cos(phase_angle)
    sine_value = jnp.sin(phase_angle)
    real_part = filtered[0] * cosine + filtered[1] * sine_value
    imag_part = filtered[1] * cosine - filtered[0] * sine_value
    return jnp.stack([real_part, imag_part]).astype(jnp.bfloat16)

def rotation_table(indices, radix_size):
    product = indices[:, None] * indices[None, :] % radix_size
    table_angle = product.astype(jnp.float32) * (2.0 * math.pi / radix_size)
    scaling = 1.0 / math.sqrt(radix_size)
    cosine = jnp.cos(table_angle) * scaling
    sine_value = jnp.sin(table_angle) * scaling
    stacked = jnp.stack([jnp.stack([cosine, sine_value], axis=1), jnp.stack([-sine_value, cosine], axis=1)], axis=0)
    return stacked.astype(jnp.bfloat16)

def dft_tables():
    along_a = jnp.arange(RADIX_A, dtype=jnp.int32)
    along_b = jnp.arange(RADIX_B, dtype=jnp.int32)
    first_table = rotation_table(along_a, RADIX_A)
    second_table = rotation_table(along_b, RADIX_B)
    product = along_a[:, None] * along_b[None, :] % CHANNELS
    twist_angle = product.astype(jnp.float32) * (2.0 * math.pi / CHANNELS)
    twiddle = jnp.stack([jnp.cos(twist_angle), jnp.sin(twist_angle)])
    return (first_table, twiddle, second_table)

def transform(rotated, tables):
    first_table, twiddle, second_table = tables
    row_count = rotated.shape[1]
    frames = rotated.shape[2] // CHANNELS
    arranged = rotated.reshape(2, row_count, frames, RADIX_A, RADIX_B)
    section_half = jnp.einsum('pkcn,crfnm->prfkm', first_table.astype(jnp.float32), arranged.astype(jnp.float32))
    real_part = section_half[0] * twiddle[0] + section_half[1] * twiddle[1]
    imag_part = section_half[1] * twiddle[0] - section_half[0] * twiddle[1]
    partial_value = jnp.stack([real_part, imag_part]).astype(jnp.bfloat16)
    spectrum = jnp.einsum('qjpm,prfkm->rfqjk', second_table.astype(jnp.float32), partial_value.astype(jnp.float32))
    return spectrum.astype(jnp.bfloat16).reshape(row_count, frames, 2, CHANNELS)

def correlate_block(spectra):
    frame_total = spectra.shape[1]
    turned = jnp.stack([-spectra[:, :, 1], spectra[:, :, 0]], axis=2)
    partner = jnp.concatenate([spectra, turned], axis=0)
    summed = jnp.einsum('ifck,jfck->kij', spectra.astype(jnp.float32), partner.astype(jnp.float32))
    return summed / frame_total

def reference(voltages, sample_delay, frac_index, phase_index, fringe_rate):
    length = FRAMES * CHANNELS
    padded = jnp.concatenate([voltages, jnp.zeros((2, SUBBANDS, STATIONS, MAXD + 128), voltages.dtype)], axis=3)
    tables = dft_tables()
    block_width = math.gcd(CHANNELS, 1024)
    results = []
    for band_index in range(SUBBANDS):
        signal = padded[:, band_index]
        phase_band = phase_index[band_index]
        rate_band = fringe_rate[band_index]

        def one_slice(slice_at, signal=signal, phase_band=phase_band, rate_band=rate_band):
            starts = (slice_at * length + sample_delay[:, slice_at]).astype(jnp.int32)
            kernel = toeplitz_of(frac_index[:, slice_at])
            filtered = filter_rows(signal, starts, kernel, length)
            rotated = rotate_rows(filtered, phase_band[:, slice_at], rate_band, 0, length)
            return transform(rotated, tables)
        spectra = lax.map(one_slice, jnp.arange(SLICES, dtype=jnp.int32))
        spectra = jnp.moveaxis(spectra, 0, 1).reshape(STATIONS, SLICES * FRAMES, 2, CHANNELS)
        blocks = jnp.moveaxis(spectra.reshape(STATIONS, SLICES * FRAMES, 2, CHANNELS // block_width, block_width), 3, 0)
        summed = lax.map(correlate_block, blocks)
        results.append(summed.reshape(CHANNELS, STATIONS, 2 * STATIONS))
    return jnp.stack(results)
```

```python
import functools
import math

import jax
import jax.numpy as jnp
import numpy as np
from jax import lax
from jax.experimental import pallas as pl
from jax.experimental.pallas import tpu as pltpu
from jax.sharding import PartitionSpec as P

CHANNELS = 16384
RADIX_A = 128
RADIX_B = 128
TAPS = 32
NFRAC = 64
NPHASE = 1024
MAXD = 8192


def shifted(value, axis, steps):
    count = lax.axis_size(axis)
    first, last = (max(0, -steps), min(count, count - steps))
    return lax.ppermute(value, axis, [(source, source + steps) for source in range(first, last)])


def toeplitz_of(fraction_index):
    inputs_at = jnp.arange(256, dtype=jnp.int32)
    outputs_at = jnp.arange(128, dtype=jnp.int32)
    distance = inputs_at[:, None] - outputs_at[None, :]
    inside = (distance >= 0) & (distance < TAPS)
    fraction = fraction_index.astype(jnp.float32) / NFRAC
    offset = distance.astype(jnp.float32)
    centre = offset[None, :, :] - (TAPS // 2 - 1) - fraction[:, None, None]
    window_taper = 0.5 - 0.5 * jnp.cos(2.0 * jnp.pi * (offset + 0.5) / TAPS)
    values = jnp.sinc(centre) * window_taper[None, :, :]
    return jnp.where(inside[None, :, :], values, 0.0).astype(jnp.bfloat16)


def filter_rows(source, starts, kernel, sample_count):
    slicer = jax.vmap(
        lambda series, start_at: lax.dynamic_slice_in_dim(
            series, start_at, sample_count + 128, axis=1
        ),
        in_axes=(1, 0),
        out_axes=1,
    )
    pieces = slicer(source, starts)
    row_count = pieces.shape[1]
    blocks = sample_count // 128
    tiles = pieces.reshape(2, row_count, blocks + 1, 128)
    upper = jnp.einsum(
        "crnp,rpv->crnv", tiles[:, :, :blocks], kernel[:, :128], preferred_element_type=jnp.float32
    )
    lower = jnp.einsum(
        "crnp,rpv->crnv", tiles[:, :, 1:], kernel[:, 128:], preferred_element_type=jnp.float32
    )
    return (upper + lower).reshape(2, row_count, sample_count)


def rotate_rows(filtered, phase_rows, rate_rows, slice_length):
    sample_count = filtered.shape[-1]
    position = jnp.arange(sample_count, dtype=jnp.int32).astype(jnp.float32) / slice_length
    cycles = (
        phase_rows.astype(jnp.float32)[:, None] / NPHASE + rate_rows[:, None] * position[None, :]
    )
    phase_angle = 2.0 * jnp.pi * cycles
    cosine = jnp.cos(phase_angle)
    sine_value = jnp.sin(phase_angle)
    real_part = filtered[0] * cosine + filtered[1] * sine_value
    imag_part = filtered[1] * cosine - filtered[0] * sine_value
    return jnp.stack([real_part, imag_part]).astype(jnp.bfloat16)


def rotation_table(indices, radix_size):
    product = indices[:, None] * indices[None, :] % radix_size
    table_angle = product.astype(jnp.float32) * (2.0 * math.pi / radix_size)
    scaling = 1.0 / math.sqrt(radix_size)
    cosine = jnp.cos(table_angle) * scaling
    sine_value = jnp.sin(table_angle) * scaling
    stacked = jnp.stack(
        [jnp.stack([cosine, sine_value], axis=1), jnp.stack([-sine_value, cosine], axis=1)], axis=0
    )
    return stacked.astype(jnp.bfloat16)


def dft_tables():
    along_a = jnp.arange(RADIX_A, dtype=jnp.int32)
    along_b = jnp.arange(RADIX_B, dtype=jnp.int32)
    first_table = rotation_table(along_a, RADIX_A)
    second_table = rotation_table(along_b, RADIX_B)
    product = along_a[:, None] * along_b[None, :] % CHANNELS
    twist_angle = product.astype(jnp.float32) * (2.0 * math.pi / CHANNELS)
    twiddle = jnp.stack([jnp.cos(twist_angle), jnp.sin(twist_angle)])
    return (first_table, twiddle, second_table)


def transform(rotated, tables, block_width):
    first_table, twiddle, second_table = tables
    row_count = rotated.shape[1]
    frames = rotated.shape[2] // CHANNELS
    arranged = rotated.reshape(2, row_count, frames, RADIX_A, RADIX_B)
    section_half = jnp.einsum(
        "pkcn,crfnm->prfkm", first_table, arranged, preferred_element_type=jnp.float32
    )
    real_part = section_half[0] * twiddle[0] + section_half[1] * twiddle[1]
    imag_part = section_half[1] * twiddle[0] - section_half[0] * twiddle[1]
    partial_value = jnp.stack([real_part, imag_part]).astype(jnp.bfloat16)
    block_count = CHANNELS // block_width
    if block_width <= RADIX_A:
        split_rows = partial_value.reshape(
            2, row_count, frames, RADIX_A // block_width, block_width, RADIX_B
        )
        spectrum = jnp.einsum(
            "qjpm,prfakm->rfjaqk", second_table, split_rows, preferred_element_type=jnp.float32
        )
    else:
        split_table = second_table.reshape(2, block_count, block_width // RADIX_A, 2, RADIX_B)
        spectrum = jnp.einsum(
            "qJjpm,prfkm->rfJqjk", split_table, partial_value, preferred_element_type=jnp.float32
        )
    return spectrum.astype(jnp.bfloat16).reshape(row_count, frames, block_count, 2 * block_width)


def correlate(spectra):
    frame_total = spectra.shape[2]
    turned = jnp.stack([-spectra[:, :, :, 1], spectra[:, :, :, 0]], axis=3)
    partner = jnp.concatenate([spectra, turned], axis=1)
    summed = jnp.einsum("bifck,bjfck->bkij", spectra, partner, preferred_element_type=jnp.float32)
    return summed / frame_total


def local_wide(voltages, sample_delay, frac_index, phase_index, fringe_rate):
    band_count = voltages.shape[1]
    station_count = voltages.shape[2]
    length = voltages.shape[3]
    frames = length // CHANNELS
    row_count = band_count * station_count
    flattened = voltages.reshape(2, row_count, length)
    delays = jnp.broadcast_to(sample_delay[:, 0][None, :], (band_count, station_count)).reshape(
        row_count
    )
    kernel = toeplitz_of(frac_index[:, 0])
    kernel_rows = jnp.broadcast_to(kernel[None], (band_count,) + kernel.shape).reshape(
        (row_count,) + kernel.shape[1:]
    )
    phase_rows = phase_index[:, :, 0].reshape(row_count)
    rate_rows = fringe_rate.reshape(row_count)
    rim_width = MAXD + TAPS - 1
    following = shifted(flattened[:, :, :rim_width], "tm", -1)
    padding = jnp.zeros((2, row_count, 129 - TAPS), flattened.dtype)
    source = jnp.concatenate([flattened, following, padding], axis=2)
    rotated = rotate_rows(
        filter_rows(source, delays, kernel_rows, length), phase_rows, rate_rows, length
    )
    slices = lax.axis_size("tm")
    groups = lax.axis_size("sta")
    block_width = CHANNELS // (slices * groups)
    spectra = transform(rotated, dft_tables(), block_width)
    packed = spectra.reshape(band_count, station_count, frames, slices, groups, 2 * block_width)
    received = lax.all_to_all(
        lax.all_to_all(packed, "tm", split_axis=3, concat_axis=2, tiled=True),
        "sta",
        split_axis=4,
        concat_axis=1,
        tiled=True,
    )
    gathered = received.reshape(band_count, station_count * groups, slices * frames, 2, block_width)
    return correlate(gathered)


ROWS = CHANNELS // 128
REACH = MAXD // 128 + 1
STRIDE = ROWS + REACH + 7
WINDOW = 384
MESH = pl.DeviceIdType.MESH


def delay_filters(frac_index, remainder):
    inputs_at = jnp.arange(WINDOW, dtype=jnp.int32)
    outputs_at = jnp.arange(128, dtype=jnp.int32)
    distance = inputs_at[None, :, None] - outputs_at[None, None, :] - remainder[:, None, None]
    inside = (distance >= 0) & (distance < TAPS)
    fraction = frac_index.astype(jnp.float32) / NFRAC
    offset = distance.astype(jnp.float32)
    centre = offset - (TAPS // 2 - 1) - fraction[:, None, None]
    window_taper = 0.5 - 0.5 * jnp.cos(2.0 * jnp.pi * (offset + 0.5) / TAPS)
    return jnp.where(inside, jnp.sinc(centre) * window_taper, 0.0).astype(jnp.bfloat16)


def phasors(phase_index, fringe_rate, length):
    starts = jnp.arange(length // 128, dtype=jnp.int32).astype(jnp.float32) * 128 / length
    within = jnp.arange(128, dtype=jnp.int32).astype(jnp.float32) / length
    start_angle = 2.0 * jnp.pi * (
        phase_index.astype(jnp.float32)[..., None] / NPHASE + fringe_rate[..., None] * starts
    )
    within_angle = 2.0 * jnp.pi * (fringe_rate[..., None] * within)
    coarse = jnp.stack([jnp.cos(start_angle), jnp.sin(start_angle)], axis=2)
    fine = jnp.stack([jnp.cos(within_angle), jnp.sin(within_angle)], axis=2)
    return coarse, fine


def station_kernel(
    whole_rows, head_ref, tail_ref, filter_ref, coarse_ref, fine_ref, first_ref, twiddle_ref,
    second_ref, out_ref, series, gathered
):
    stations = head_ref.shape[2]

    for part in range(2):
        for row in range(ROWS + REACH):
            if row < ROWS:
                tile = head_ref[part, 0, :, row * 128 : (row + 1) * 128]
            else:
                tile = tail_ref[part, 0, :, (row - ROWS) * 128 : (row - ROWS + 1) * 128]
            series[part, pl.ds(row, stations, stride=STRIDE), :] = tile.astype(jnp.float32)
        series[part, pl.ds(ROWS + REACH, stations, stride=STRIDE), :] = jnp.zeros(
            (stations, 128), jnp.float32
        )

    def across(row):
        return jnp.transpose(jnp.broadcast_to(row, (128, 128)))

    def one(station):
        base = station * STRIDE + whole_rows[station]
        parts = []
        for part in range(2):
            pieces = [
                series[part, pl.ds(base + step, ROWS), :].astype(jnp.bfloat16) for step in range(3)
            ]
            parts.append(jnp.concatenate(pieces, axis=1))
        filtered = jnp.dot(
            jnp.concatenate(parts, axis=0), filter_ref[station], preferred_element_type=jnp.float32
        )
        coarse = coarse_ref[0, station]
        fine = fine_ref[0, station]
        cos_a, sin_a = across(coarse[0:1]), across(coarse[1:2])
        cos_b, sin_b = fine[0:1], fine[1:2]
        cosine = cos_a * cos_b - sin_a * sin_b
        sine = sin_a * cos_b + cos_a * sin_b
        re, im = filtered[:ROWS], filtered[ROWS:]
        return jnp.concatenate(
            [re * cosine + im * sine, im * cosine - re * sine], axis=0
        ).astype(jnp.bfloat16)

    def pair(at, carry):
        rotated = jnp.concatenate([one(2 * at), one(2 * at + 1)], axis=1)
        half = jnp.dot(first_ref[...], rotated, preferred_element_type=jnp.float32)
        cosine, sine = twiddle_ref[0], twiddle_ref[1]
        turned = []
        for which in range(2):
            re = half[:RADIX_A, which * 128 : (which + 1) * 128]
            im = half[RADIX_A:, which * 128 : (which + 1) * 128]
            turned.append(
                jnp.concatenate([re * cosine + im * sine, im * cosine - re * sine], axis=1)
            )
        partial_value = jnp.concatenate(turned, axis=0).astype(jnp.bfloat16)
        spectrum = lax.dot_general(
            second_ref[...], partial_value, (((1,), (1,)), ((), ())),
            preferred_element_type=jnp.float32,
        )
        for which in range(2):
            gathered[pl.ds(2 * at + which, 2 * RADIX_B, stride=stations), :] = spectrum[
                :, which * 128 : (which + 1) * 128
            ]
        return carry

    lax.fori_loop(0, stations // 2, pair, 0)
    blocks, inner = out_ref.shape[1], out_ref.shape[2]

    def pack(block, carry):
        rows = pl.ds(pl.multiple_of(block * inner, inner), inner)
        out_ref[0, block] = gathered[rows, :].astype(jnp.bfloat16)
        return carry

    lax.fori_loop(0, blocks, pack, 0)


def station_spectra(frame, voltages, tail, filters, coarse, fine, tables, whole_rows, blocks):
    _, bands, stations, _ = voltages.shape
    first, twiddle, second = tables
    inner = 2 * RADIX_B // blocks * stations
    whole = lambda shape: pl.BlockSpec(shape, lambda band, rows: (0,) * len(shape))
    return pl.pallas_call(
        station_kernel,
        out_shape=jax.ShapeDtypeStruct((bands, blocks, inner, 128), jnp.bfloat16),
        grid_spec=pltpu.PrefetchScalarGridSpec(
            num_scalar_prefetch=1,
            grid=(bands,),
            in_specs=[
                pl.BlockSpec((2, 1, stations, CHANNELS), lambda band, rows: (0, band, 0, frame)),
                pl.BlockSpec((2, 1, stations, REACH * 128), lambda band, rows: (0, band, 0, 0)),
                whole(filters.shape),
                pl.BlockSpec((1, stations, 2, 128), lambda band, rows: (band, 0, 0, frame)),
                pl.BlockSpec((1, stations, 2, 128), lambda band, rows: (band, 0, 0, 0)),
                whole(first.shape),
                whole(twiddle.shape),
                whole(second.shape),
            ],
            out_specs=pl.BlockSpec((1, blocks, inner, 128), lambda band, rows: (band, 0, 0, 0)),
            scratch_shapes=[
                pltpu.VMEM((2, stations * STRIDE, 128), jnp.float32),
                pltpu.VMEM((2 * RADIX_B * stations, 128), jnp.float32),
            ],
        ),
        compiler_params=pltpu.CompilerParams(vmem_limit_bytes=48 * 2**20),
        cost_estimate=pl.CostEstimate(
            flops=4 * 10**9, bytes_accessed=10 * 2**20, transcendentals=0
        ),
    )(whole_rows, voltages, tail, filters, coarse, fine, first, twiddle, second)


def exchange_kernel(sent_ref, got_ref, send_sem, recv_sem, own_sem):
    times, groups = lax.axis_size("tm"), lax.axis_size("sta")
    count = times * groups
    at_time, at_group = lax.axis_index("tm"), lax.axis_index("sta")
    me = at_time * groups + at_group
    chunks = sent_ref.shape[0]
    barrier = pltpu.get_barrier_semaphore()

    def greet(step, carry):
        other = lax.rem(me + step, count)
        pl.semaphore_signal(
            barrier, inc=1, device_id=(other // groups, lax.rem(other, groups)),
            device_id_type=MESH,
        )
        return carry

    lax.fori_loop(1, count, greet, 0)
    pl.semaphore_wait(barrier, count - 1)
    own = pltpu.make_async_copy(sent_ref.at[:, me], got_ref.at[:, me], own_sem)
    own.start()
    for chunk in range(chunks):

        def send(step, carry, chunk=chunk):
            other = lax.rem(me + step, count)
            pltpu.make_async_remote_copy(
                src_ref=sent_ref.at[chunk, other],
                dst_ref=got_ref.at[chunk, me],
                send_sem=send_sem.at[chunk],
                recv_sem=recv_sem.at[chunk],
                device_id=(other // groups, lax.rem(other, groups)),
                device_id_type=MESH,
            ).start()
            return carry

        lax.fori_loop(1, count, send, 0)
    for chunk in range(chunks):
        every = pltpu.make_async_remote_copy(
            src_ref=sent_ref.at[chunk, pl.ds(0, count - 1)],
            dst_ref=got_ref.at[chunk, pl.ds(0, count - 1)],
            send_sem=send_sem.at[chunk],
            recv_sem=recv_sem.at[chunk],
            device_id=(at_time, at_group),
            device_id_type=MESH,
        )
        every.wait_send()
        every.wait_recv()
    own.wait()


def exchange(sent, collective):
    return pl.pallas_call(
        exchange_kernel,
        out_shape=jax.ShapeDtypeStruct(sent.shape, sent.dtype),
        in_specs=[pl.BlockSpec(memory_space=pl.ANY)],
        out_specs=pl.BlockSpec(memory_space=pl.ANY),
        scratch_shapes=[
            pltpu.SemaphoreType.DMA((sent.shape[0],)),
            pltpu.SemaphoreType.DMA((sent.shape[0],)),
            pltpu.SemaphoreType.DMA,
        ],
        compiler_params=pltpu.CompilerParams(collective_id=collective, has_side_effects=True),
        cost_estimate=pl.CostEstimate(
            flops=0, bytes_accessed=300 * 2**20, transcendentals=0
        ),
    )(sent)


def correlate_kernel(scale, *refs):
    frame_refs, out_ref, turned = refs[:-2], refs[-2], refs[-1]
    times, groups = frame_refs[0].shape[1], frame_refs[0].shape[2]
    depth = 2 * times * len(frame_refs)
    stations = groups * frame_refs[0].shape[5]
    lane = lax.broadcasted_iota(jnp.int32, (128, 128), 1)
    sign = jnp.where(lane < stations, 1.0, -1.0)
    at = 0
    for ref in frame_refs:
        for time in range(times):
            both = [
                ref[0, time, group, 0, part] for part in range(2) for group in range(groups)
            ]
            tile = jnp.transpose(jnp.concatenate(both, axis=0).astype(jnp.float32))
            turned[pl.ds(at, 128, stride=depth), :] = tile * sign
            turned[pl.ds(depth // 2 + at, 128, stride=depth), :] = pltpu.roll(tile, stations, 1)
            at += 1
    many = 128 // depth

    def step(group, carry):
        rows = pl.ds(pl.multiple_of(group * 128, 128), 128)
        block = turned[rows, :]
        left = jnp.transpose(block)[:stations].astype(jnp.bfloat16)
        narrow = block.astype(jnp.bfloat16)
        columns = []
        for one in range(many):
            pieces = []
            if one:
                pieces.append(jnp.zeros((one * depth, 128), jnp.bfloat16))
            pieces.append(narrow[one * depth : (one + 1) * depth])
            if one < many - 1:
                pieces.append(jnp.zeros(((many - 1 - one) * depth, 128), jnp.bfloat16))
            columns.append(jnp.concatenate(pieces, axis=0))
        result = jnp.dot(
            left, jnp.concatenate(columns, axis=1), preferred_element_type=jnp.float32
        )
        for one in range(many):
            out_ref[0, group * many + one] = result[:, one * 128 : (one + 1) * 128] * scale
        return carry

    lax.fori_loop(0, 128 // many, step, 0, unroll=4)


def correlate_frames(frames, times, groups, stations):
    bands, _, inner, _ = frames[0].shape
    columns = inner // (2 * stations)
    depth = 2 * times * len(frames)
    shaped = [
        frame.reshape(bands, times, groups, columns, 2, stations, 128) for frame in frames
    ]
    total = groups * stations
    return pl.pallas_call(
        functools.partial(correlate_kernel, 2.0 / depth),
        out_shape=jax.ShapeDtypeStruct((bands, columns * 128, total, 2 * total), jnp.float32),
        grid=(bands, columns),
        in_specs=[
            pl.BlockSpec(
                (1, times, groups, 1, 2, stations, 128),
                lambda band, column: (band, 0, 0, column, 0, 0, 0),
            )
            for _ in frames
        ],
        out_specs=pl.BlockSpec(
            (1, 128, total, 2 * total), lambda band, column: (band, column, 0, 0)
        ),
        scratch_shapes=[pltpu.VMEM((128 * depth, 128), jnp.float32)],
        compiler_params=pltpu.CompilerParams(vmem_limit_bytes=32 * 2**20),
    )(*shaped)


def flat_tables():
    first, twiddle, second = dft_tables()
    first = first.reshape(2 * RADIX_A, 2 * RADIX_A)
    second = jnp.transpose(second, (1, 0, 2, 3)).reshape(2 * RADIX_B, 2 * RADIX_B)
    return first, twiddle, second


def local_narrow(voltages, sample_delay, frac_index, phase_index, fringe_rate):
    stations, length = voltages.shape[2], voltages.shape[3]
    times, groups = lax.axis_size("tm"), lax.axis_size("sta")
    reach = REACH * 128
    following = shifted(voltages[..., :reach], "tm", -1)
    delay = sample_delay[:, 0]
    filters = delay_filters(frac_index[:, 0], delay % 128)
    coarse, fine = phasors(phase_index[:, :, 0], fringe_rate, length)
    tables = flat_tables()
    received = []
    for frame in range(length // CHANNELS):
        end = (frame + 1) * CHANNELS
        tail = voltages[..., end : end + reach] if end + reach <= length else following
        sent = station_spectra(
            frame, voltages, tail, filters, coarse, fine, tables, delay // 128, times * groups
        )
        received.append(exchange(sent, frame))
    return correlate_frames(received, times, groups, stations)


def local(voltages, *others):
    stations = voltages.shape[2] * lax.axis_size("sta")
    block_width = CHANNELS // (lax.axis_size("tm") * lax.axis_size("sta"))
    depth = 2 * lax.axis_size("tm") * (voltages.shape[3] // CHANNELS)
    fits = voltages.shape[2] % 16 == 0 and block_width % 128 == 0 and depth <= 64
    if fits and stations == 64:
        return local_narrow(voltages, *others)
    return local_wide(voltages, *others)


def solution(mesh):
    return jax.shard_map(
        local,
        mesh=mesh,
        in_specs=(
            P(None, None, "sta", "tm"),
            P("sta", "tm"),
            P("sta", "tm"),
            P(None, "sta", "tm"),
            P(None, "sta"),
        ),
        out_specs=P(None, ("tm", "sta"), None, None),
        check_vma=False,
    )
```

```python
import functools
import math

import jax
import jax.numpy as jnp
import numpy as np
from jax import lax
from jax.experimental import pallas as pl
from jax.experimental.pallas import tpu as pltpu
from jax.sharding import PartitionSpec as P

CHANNELS = 16384
RADIX_A = 128
RADIX_B = 128
TAPS = 32
NFRAC = 64
NPHASE = 1024
MAXD = 8192


def shifted(value, axis, steps):
    count = lax.axis_size(axis)
    first, last = (max(0, -steps), min(count, count - steps))
    return lax.ppermute(value, axis, [(source, source + steps) for source in range(first, last)])


def toeplitz_of(fraction_index):
    inputs_at = jnp.arange(256, dtype=jnp.int32)
    outputs_at = jnp.arange(128, dtype=jnp.int32)
    distance = inputs_at[:, None] - outputs_at[None, :]
    inside = (distance >= 0) & (distance < TAPS)
    fraction = fraction_index.astype(jnp.float32) / NFRAC
    offset = distance.astype(jnp.float32)
    centre = offset[None, :, :] - (TAPS // 2 - 1) - fraction[:, None, None]
    window_taper = 0.5 - 0.5 * jnp.cos(2.0 * jnp.pi * (offset + 0.5) / TAPS)
    values = jnp.sinc(centre) * window_taper[None, :, :]
    return jnp.where(inside[None, :, :], values, 0.0).astype(jnp.bfloat16)


def filter_rows(source, starts, kernel, sample_count):
    slicer = jax.vmap(
        lambda series, start_at: lax.dynamic_slice_in_dim(
            series, start_at, sample_count + 128, axis=1
        ),
        in_axes=(1, 0),
        out_axes=1,
    )
    pieces = slicer(source, starts)
    row_count = pieces.shape[1]
    blocks = sample_count // 128
    tiles = pieces.reshape(2, row_count, blocks + 1, 128)
    upper = jnp.einsum(
        "crnp,rpv->crnv", tiles[:, :, :blocks], kernel[:, :128], preferred_element_type=jnp.float32
    )
    lower = jnp.einsum(
        "crnp,rpv->crnv", tiles[:, :, 1:], kernel[:, 128:], preferred_element_type=jnp.float32
    )
    return (upper + lower).reshape(2, row_count, sample_count)


def rotate_rows(filtered, phase_rows, rate_rows, slice_length):
    sample_count = filtered.shape[-1]
    position = jnp.arange(sample_count, dtype=jnp.int32).astype(jnp.float32) / slice_length
    cycles = (
        phase_rows.astype(jnp.float32)[:, None] / NPHASE + rate_rows[:, None] * position[None, :]
    )
    phase_angle = 2.0 * jnp.pi * cycles
    cosine = jnp.cos(phase_angle)
    sine_value = jnp.sin(phase_angle)
    real_part = filtered[0] * cosine + filtered[1] * sine_value
    imag_part = filtered[1] * cosine - filtered[0] * sine_value
    return jnp.stack([real_part, imag_part]).astype(jnp.bfloat16)


def rotation_table(indices, radix_size):
    product = indices[:, None] * indices[None, :] % radix_size
    table_angle = product.astype(jnp.float32) * (2.0 * math.pi / radix_size)
    scaling = 1.0 / math.sqrt(radix_size)
    cosine = jnp.cos(table_angle) * scaling
    sine_value = jnp.sin(table_angle) * scaling
    stacked = jnp.stack(
        [jnp.stack([cosine, sine_value], axis=1), jnp.stack([-sine_value, cosine], axis=1)], axis=0
    )
    return stacked.astype(jnp.bfloat16)


def dft_tables():
    along_a = jnp.arange(RADIX_A, dtype=jnp.int32)
    along_b = jnp.arange(RADIX_B, dtype=jnp.int32)
    first_table = rotation_table(along_a, RADIX_A)
    second_table = rotation_table(along_b, RADIX_B)
    product = along_a[:, None] * along_b[None, :] % CHANNELS
    twist_angle = product.astype(jnp.float32) * (2.0 * math.pi / CHANNELS)
    twiddle = jnp.stack([jnp.cos(twist_angle), jnp.sin(twist_angle)])
    return (first_table, twiddle, second_table)


def transform(rotated, tables, block_width):
    first_table, twiddle, second_table = tables
    row_count = rotated.shape[1]
    frames = rotated.shape[2] // CHANNELS
    arranged = rotated.reshape(2, row_count, frames, RADIX_A, RADIX_B)
    section_half = jnp.einsum(
        "pkcn,crfnm->prfkm", first_table, arranged, preferred_element_type=jnp.float32
    )
    real_part = section_half[0] * twiddle[0] + section_half[1] * twiddle[1]
    imag_part = section_half[1] * twiddle[0] - section_half[0] * twiddle[1]
    partial_value = jnp.stack([real_part, imag_part]).astype(jnp.bfloat16)
    block_count = CHANNELS // block_width
    if block_width <= RADIX_A:
        split_rows = partial_value.reshape(
            2, row_count, frames, RADIX_A // block_width, block_width, RADIX_B
        )
        spectrum = jnp.einsum(
            "qjpm,prfakm->rfjaqk", second_table, split_rows, preferred_element_type=jnp.float32
        )
    else:
        split_table = second_table.reshape(2, block_count, block_width // RADIX_A, 2, RADIX_B)
        spectrum = jnp.einsum(
            "qJjpm,prfkm->rfJqjk", split_table, partial_value, preferred_element_type=jnp.float32
        )
    return spectrum.astype(jnp.bfloat16).reshape(row_count, frames, block_count, 2 * block_width)


def correlate(spectra):
    frame_total = spectra.shape[2]
    turned = jnp.stack([-spectra[:, :, :, 1], spectra[:, :, :, 0]], axis=3)
    partner = jnp.concatenate([spectra, turned], axis=1)
    summed = jnp.einsum("bifck,bjfck->bkij", spectra, partner, preferred_element_type=jnp.float32)
    return summed / frame_total


def local_wide(voltages, sample_delay, frac_index, phase_index, fringe_rate):
    band_count = voltages.shape[1]
    station_count = voltages.shape[2]
    length = voltages.shape[3]
    frames = length // CHANNELS
    row_count = band_count * station_count
    flattened = voltages.reshape(2, row_count, length)
    delays = jnp.broadcast_to(sample_delay[:, 0][None, :], (band_count, station_count)).reshape(
        row_count
    )
    kernel = toeplitz_of(frac_index[:, 0])
    kernel_rows = jnp.broadcast_to(kernel[None], (band_count,) + kernel.shape).reshape(
        (row_count,) + kernel.shape[1:]
    )
    phase_rows = phase_index[:, :, 0].reshape(row_count)
    rate_rows = fringe_rate.reshape(row_count)
    rim_width = MAXD + TAPS - 1
    following = shifted(flattened[:, :, :rim_width], "tm", -1)
    padding = jnp.zeros((2, row_count, 129 - TAPS), flattened.dtype)
    source = jnp.concatenate([flattened, following, padding], axis=2)
    rotated = rotate_rows(
        filter_rows(source, delays, kernel_rows, length), phase_rows, rate_rows, length
    )
    slices = lax.axis_size("tm")
    groups = lax.axis_size("sta")
    block_width = CHANNELS // (slices * groups)
    spectra = transform(rotated, dft_tables(), block_width)
    packed = spectra.reshape(band_count, station_count, frames, slices, groups, 2 * block_width)
    received = lax.all_to_all(
        lax.all_to_all(packed, "tm", split_axis=3, concat_axis=2, tiled=True),
        "sta",
        split_axis=4,
        concat_axis=1,
        tiled=True,
    )
    gathered = received.reshape(band_count, station_count * groups, slices * frames, 2, block_width)
    return correlate(gathered)


ROWS = CHANNELS // 128
REACH = MAXD // 128 + 1
STRIDE = ROWS + REACH + 7
WINDOW = 384
ABOVE = 128
TALL = ABOVE + WINDOW
MESH = pl.DeviceIdType.MESH


def delay_filters(frac_index):
    kernel = toeplitz_of(frac_index)[:, : 128 + TAPS].astype(jnp.float32)
    kernel = jnp.pad(kernel, ((0, 0), (ABOVE, TALL - ABOVE - 128 - TAPS), (0, 0)))
    return kernel.reshape(-1, 128)


def phasors(phase_index, fringe_rate, length):
    starts = jnp.arange(length // 128, dtype=jnp.int32).astype(jnp.float32) * 128 / length
    within = jnp.arange(128, dtype=jnp.int32).astype(jnp.float32) / length
    start_angle = 2.0 * jnp.pi * (
        phase_index.astype(jnp.float32)[..., None] / NPHASE + fringe_rate[..., None] * starts
    )
    within_angle = 2.0 * jnp.pi * (fringe_rate[..., None] * within)
    coarse = jnp.stack([jnp.cos(start_angle), jnp.sin(start_angle)], axis=2)
    fine = jnp.stack([jnp.cos(within_angle), jnp.sin(within_angle)], axis=2)
    return coarse, fine


def station_band(
    shifts, read_head, read_tail, filter_ref, read_coarse, read_fine, first_ref, twiddle_ref,
    second_ref, write, stations, blocks, series, gathered
):
    for part in range(2):
        for row in range(ROWS + REACH):
            tile = read_head(part, row) if row < ROWS else read_tail(part, row - ROWS)
            series[part, pl.ds(row, stations, stride=STRIDE), :] = tile.astype(jnp.float32)
        series[part, pl.ds(ROWS + REACH, stations, stride=STRIDE), :] = jnp.zeros(
            (stations, 128), jnp.float32
        )

    def across(row):
        return jnp.transpose(jnp.broadcast_to(row, (128, 128)))

    def one(station):
        base = station * STRIDE + shifts[0, station]
        parts = []
        for part in range(2):
            pieces = [
                series[part, pl.ds(base + step, ROWS), :].astype(jnp.bfloat16) for step in range(3)
            ]
            parts.append(jnp.concatenate(pieces, axis=1))
        taps = filter_ref[pl.ds(station * TALL + ABOVE - shifts[1, station], WINDOW), :]
        filtered = jnp.dot(
            jnp.concatenate(parts, axis=0), taps.astype(jnp.bfloat16),
            preferred_element_type=jnp.float32,
        )
        coarse = read_coarse(station)
        fine = read_fine(station)
        cos_a, sin_a = across(coarse[0:1]), across(coarse[1:2])
        cos_b, sin_b = fine[0:1], fine[1:2]
        cosine = cos_a * cos_b - sin_a * sin_b
        sine = sin_a * cos_b + cos_a * sin_b
        re, im = filtered[:ROWS], filtered[ROWS:]
        return jnp.concatenate(
            [re * cosine + im * sine, im * cosine - re * sine], axis=0
        ).astype(jnp.bfloat16)

    def pair(at, carry):
        rotated = jnp.concatenate([one(2 * at), one(2 * at + 1)], axis=1)
        half = jnp.dot(first_ref[...], rotated, preferred_element_type=jnp.float32)
        cosine, sine = twiddle_ref[0], twiddle_ref[1]
        turned = []
        for which in range(2):
            re = half[:RADIX_A, which * 128 : (which + 1) * 128]
            im = half[RADIX_A:, which * 128 : (which + 1) * 128]
            turned.append(
                jnp.concatenate([re * cosine + im * sine, im * cosine - re * sine], axis=1)
            )
        partial_value = jnp.concatenate(turned, axis=0).astype(jnp.bfloat16)
        spectrum = lax.dot_general(
            second_ref[...], partial_value, (((1,), (1,)), ((), ())),
            preferred_element_type=jnp.float32,
        )
        for which in range(2):
            gathered[pl.ds(2 * at + which, 2 * RADIX_B, stride=stations), :] = spectrum[
                :, which * 128 : (which + 1) * 128
            ]
        return carry

    lax.fori_loop(0, stations // 2, pair, 0)
    inner = 2 * RADIX_B // blocks * stations

    def pack(block, carry):
        rows = pl.ds(pl.multiple_of(block * inner, inner), inner)
        write(block, gathered[rows, :].astype(jnp.bfloat16))
        return carry

    lax.fori_loop(0, blocks, pack, 0)


def columns_of(row):
    return slice(row * 128, (row + 1) * 128)


def station_kernel(
    shifts, head_ref, tail_ref, filter_ref, coarse_ref, fine_ref, first_ref, twiddle_ref,
    second_ref, out_ref, series, gathered
):
    def write(block, value):
        out_ref[0, block] = value

    station_band(
        shifts,
        lambda part, row: head_ref[part, 0, :, columns_of(row)],
        lambda part, row: tail_ref[part, 0, :, columns_of(row)],
        filter_ref,
        lambda station: coarse_ref[0, station],
        lambda station: fine_ref[0, station],
        first_ref, twiddle_ref, second_ref, write,
        head_ref.shape[2], out_ref.shape[1], series, gathered,
    )


def station_scratch(stations):
    return [
        pltpu.VMEM((2, stations * STRIDE, 128), jnp.float32),
        pltpu.VMEM((2 * RADIX_B * stations, 128), jnp.float32),
    ]


def station_spectra(voltages, shifts, tail, filters, coarse, fine, tables, blocks):
    _, bands, stations, _ = voltages.shape
    first, twiddle, second = tables
    inner = 2 * RADIX_B // blocks * stations
    whole = lambda shape: pl.BlockSpec(shape, lambda band, rows: (0,) * len(shape))
    return pl.pallas_call(
        station_kernel,
        out_shape=jax.ShapeDtypeStruct((bands, blocks, inner, 128), jnp.bfloat16),
        grid_spec=pltpu.PrefetchScalarGridSpec(
            num_scalar_prefetch=1,
            grid=(bands,),
            in_specs=[
                pl.BlockSpec((2, 1, stations, CHANNELS), lambda band, rows: (0, band, 0, 0)),
                pl.BlockSpec((2, 1, stations, REACH * 128), lambda band, rows: (0, band, 0, 0)),
                whole(filters.shape),
                pl.BlockSpec((1, stations, 2, 128), lambda band, rows: (band, 0, 0, 0)),
                pl.BlockSpec((1, stations, 2, 128), lambda band, rows: (band, 0, 0, 0)),
                whole(first.shape),
                whole(twiddle.shape),
                whole(second.shape),
            ],
            out_specs=pl.BlockSpec((1, blocks, inner, 128), lambda band, rows: (band, 0, 0, 0)),
            scratch_shapes=station_scratch(stations),
        ),
        compiler_params=pltpu.CompilerParams(vmem_limit_bytes=48 * 2**20),
        cost_estimate=pl.CostEstimate(
            flops=4 * 10**9, bytes_accessed=10 * 2**20, transcendentals=0
        ),
    )(shifts, voltages, tail, filters, coarse, fine, first, twiddle, second)


def stream_kernel(
    shifts, voltages_ref, tail_ref, sent_ref, filter_ref, coarse_ref, fine_ref, first_ref,
    twiddle_ref, second_ref, got_ref, last_ref, heads, tails, ready, series, gathered,
    send_sem, recv_sem, own_sem, load_sem
):
    times, groups = lax.axis_size("tm"), lax.axis_size("sta")
    count = times * groups
    at_time, at_group = lax.axis_index("tm"), lax.axis_index("sta")
    me = at_time * groups + at_group
    bands = sent_ref.shape[0]
    stations = heads.shape[2]
    barrier = pltpu.get_barrier_semaphore()

    def greet(step, carry):
        other = lax.rem(me + step, count)
        pl.semaphore_signal(
            barrier, inc=1, device_id=(other // groups, lax.rem(other, groups)),
            device_id_type=MESH,
        )
        return carry

    load_head = pltpu.make_async_copy(
        voltages_ref.at[:, :, :, pl.ds(CHANNELS, CHANNELS)], heads, load_sem.at[0]
    )
    load_tail = pltpu.make_async_copy(tail_ref, tails, load_sem.at[1])
    load_head.start()
    load_tail.start()
    lax.fori_loop(1, count, greet, 0)
    pl.semaphore_wait(barrier, count - 1)

    def copy_to(other, source, target, chunk):
        return pltpu.make_async_remote_copy(
            src_ref=source,
            dst_ref=target,
            send_sem=send_sem.at[chunk],
            recv_sem=recv_sem.at[chunk],
            device_id=(other // groups, lax.rem(other, groups)),
            device_id_type=MESH,
        )

    def send_all(source, target, band, chunk):
        def send(step, carry):
            other = lax.rem(me + step, count)
            copy_to(other, source.at[band, other], target.at[band, me], chunk).start()
            return carry

        lax.fori_loop(1, count, send, 0)

    def first_frame(band, carry):
        send_all(sent_ref, got_ref, band, band)
        return carry

    lax.fori_loop(0, bands, first_frame, 0)
    own = pltpu.make_async_copy(sent_ref.at[:, me], got_ref.at[:, me], own_sem.at[0])
    own.start()
    load_head.wait()
    load_tail.wait()

    def second_frame(band, carry):
        def write(block, value):
            ready[band, block] = value

        station_band(
            shifts,
            lambda part, row: heads[part, band, :, columns_of(row)],
            lambda part, row: tails[part, band, :, columns_of(row)],
            filter_ref,
            lambda station: coarse_ref[band, station],
            lambda station: fine_ref[band, station],
            first_ref, twiddle_ref, second_ref, write,
            stations, count, series, gathered,
        )
        send_all(ready, last_ref, band, bands + band)
        return carry

    lax.fori_loop(0, bands, second_frame, 0)
    own_last = pltpu.make_async_copy(ready.at[:, me], last_ref.at[:, me], own_sem.at[1])
    own_last.start()
    for chunk in range(2 * bands):
        source, target = (sent_ref, got_ref) if chunk < bands else (ready, last_ref)
        every = pltpu.make_async_remote_copy(
            src_ref=source.at[chunk % bands, pl.ds(0, count - 1)],
            dst_ref=target.at[chunk % bands, pl.ds(0, count - 1)],
            send_sem=send_sem.at[chunk],
            recv_sem=recv_sem.at[chunk],
            device_id=(at_time, at_group),
            device_id_type=MESH,
        )
        every.wait_send()
        every.wait_recv()
    own.wait()
    own_last.wait()


def stream(shifts, voltages, tail, sent, filters, coarse, fine, tables):
    _, bands, stations, _ = voltages.shape
    inside = pl.BlockSpec(memory_space=pltpu.VMEM)
    outside = pl.BlockSpec(memory_space=pl.ANY)
    shape = jax.ShapeDtypeStruct(sent.shape, sent.dtype)
    return pl.pallas_call(
        stream_kernel,
        out_shape=(shape, shape),
        in_specs=[pl.BlockSpec(memory_space=pltpu.SMEM)] + [outside] * 3 + [inside] * 6,
        out_specs=(outside, outside),
        scratch_shapes=[
            pltpu.VMEM((2, bands, stations, CHANNELS), voltages.dtype),
            pltpu.VMEM(tail.shape, tail.dtype),
            pltpu.VMEM(sent.shape, sent.dtype),
        ]
        + station_scratch(stations)
        + [
            pltpu.SemaphoreType.DMA((2 * bands,)),
            pltpu.SemaphoreType.DMA((2 * bands,)),
            pltpu.SemaphoreType.DMA((2,)),
            pltpu.SemaphoreType.DMA((2,)),
        ],
        compiler_params=pltpu.CompilerParams(
            collective_id=0, has_side_effects=True, vmem_limit_bytes=48 * 2**20
        ),
        cost_estimate=pl.CostEstimate(
            flops=4 * 10**9, bytes_accessed=600 * 2**20, transcendentals=0
        ),
    )(shifts, voltages, tail, sent, filters, coarse, fine, *tables)


def correlate_kernel(scale, *refs):
    frame_refs, out_ref, turned = refs[:-2], refs[-2], refs[-1]
    times, groups = frame_refs[0].shape[1], frame_refs[0].shape[2]
    frames = times * len(frame_refs)
    stations = groups * frame_refs[0].shape[5]
    stride = frames + 8
    at = 0
    for ref in frame_refs:
        for time in range(times):
            both = [
                ref[0, time, group, 0, part] for part in range(2) for group in range(groups)
            ]
            turned[pl.ds(at, 128, stride=stride), :] = jnp.transpose(
                jnp.concatenate(both, axis=0).astype(jnp.float32)
            )
            at += 1
    many = 128 // frames
    lane = lax.broadcasted_iota(jnp.int32, (128, 128), 1)
    sign = jnp.where(lane < stations, 1.0, -1.0).astype(jnp.bfloat16)
    owner = lax.broadcasted_iota(jnp.int32, (stations, 256), 1) % 128 // frames

    def step(group, carry):
        block = jnp.concatenate(
            [
                turned[pl.ds(pl.multiple_of((group * many + one) * stride, 8), frames), :]
                for one in range(many)
            ],
            axis=0,
        ).astype(jnp.bfloat16)
        flipped = jnp.transpose(block)
        left = jnp.concatenate([flipped[:stations], flipped[stations:]], axis=1)
        swapped = jnp.concatenate([block[:, stations:], block[:, :stations]], axis=1)
        right = jnp.concatenate([block * sign, swapped], axis=0)
        spread = jnp.concatenate(
            [jnp.where(owner == one, left, jnp.zeros_like(left)) for one in range(many)], axis=0
        )
        result = jnp.dot(spread, right, preferred_element_type=jnp.float32)
        for one in range(many):
            out_ref[0, group * many + one] = result[one * stations : (one + 1) * stations] * scale
        return carry

    lax.fori_loop(0, 128 // many, step, 0, unroll=True)


def correlate_frames(frames, times, groups, stations):
    bands, _, inner, _ = frames[0].shape
    columns = inner // (2 * stations)
    depth = 2 * times * len(frames)
    shaped = [
        frame.reshape(bands, times, groups, columns, 2, stations, 128) for frame in frames
    ]
    total = groups * stations
    return pl.pallas_call(
        functools.partial(correlate_kernel, 2.0 / depth),
        out_shape=jax.ShapeDtypeStruct((bands, columns * 128, total, 2 * total), jnp.float32),
        grid=(bands, columns),
        in_specs=[
            pl.BlockSpec(
                (1, times, groups, 1, 2, stations, 128),
                lambda band, column: (band, 0, 0, column, 0, 0, 0),
            )
            for _ in frames
        ],
        out_specs=pl.BlockSpec(
            (1, 128, total, 2 * total), lambda band, column: (band, column, 0, 0)
        ),
        scratch_shapes=[pltpu.VMEM((128 * (depth // 2 + 8), 128), jnp.float32)],
        compiler_params=pltpu.CompilerParams(vmem_limit_bytes=32 * 2**20),
    )(*shaped)


def flat_tables():
    first, twiddle, second = dft_tables()
    first = first.reshape(2 * RADIX_A, 2 * RADIX_A)
    second = jnp.transpose(second, (1, 0, 2, 3)).reshape(2 * RADIX_B, 2 * RADIX_B)
    return first, twiddle, second


def local_narrow(voltages, sample_delay, frac_index, phase_index, fringe_rate):
    length = voltages.shape[3]
    times, groups = lax.axis_size("tm"), lax.axis_size("sta")
    reach = REACH * 128
    following = shifted(voltages[..., :reach], "tm", -1)
    delay = sample_delay[:, 0]
    shifts = jnp.stack([delay // 128, delay % 128])
    filters = delay_filters(frac_index[:, 0])
    coarse, fine = phasors(phase_index[:, :, 0], fringe_rate, length)
    tables = flat_tables()
    middle = voltages[..., CHANNELS : CHANNELS + reach]
    early, late = coarse[..., :ROWS], coarse[..., ROWS:]
    sent = station_spectra(
        voltages, shifts, middle, filters, early, fine, tables, times * groups
    )
    received = stream(shifts, voltages, following, sent, filters, late, fine, tables)
    return correlate_frames(received, times, groups, voltages.shape[2])


def local(voltages, *others):
    stations = voltages.shape[2] * lax.axis_size("sta")
    block_width = CHANNELS // (lax.axis_size("tm") * lax.axis_size("sta"))
    depth = 2 * lax.axis_size("tm") * (voltages.shape[3] // CHANNELS)
    fits = voltages.shape[2] % 16 == 0 and block_width % 128 == 0 and depth == 32
    if fits and stations == 64 and voltages.shape[3] == 2 * CHANNELS:
        return local_narrow(voltages, *others)
    return local_wide(voltages, *others)


def solution(mesh):
    return jax.shard_map(
        local,
        mesh=mesh,
        in_specs=(
            P(None, None, "sta", "tm"),
            P("sta", "tm"),
            P("sta", "tm"),
            P(None, "sta", "tm"),
            P(None, "sta"),
        ),
        out_specs=P(None, ("tm", "sta"), None, None),
        check_vma=False,
    )
```

```python
import functools
import math

import jax
import jax.numpy as jnp
import numpy as np
from jax import lax
from jax.experimental import pallas as pl
from jax.experimental.pallas import tpu as pltpu
from jax.sharding import PartitionSpec as P

CHANNELS = 16384
RADIX_A = 128
RADIX_B = 128
TAPS = 32
NFRAC = 64
NPHASE = 1024
MAXD = 8192


def shifted(value, axis, steps):
    count = lax.axis_size(axis)
    first, last = (max(0, -steps), min(count, count - steps))
    return lax.ppermute(value, axis, [(source, source + steps) for source in range(first, last)])


def toeplitz_of(fraction_index):
    inputs_at = jnp.arange(256, dtype=jnp.int32)
    outputs_at = jnp.arange(128, dtype=jnp.int32)
    distance = inputs_at[:, None] - outputs_at[None, :]
    inside = (distance >= 0) & (distance < TAPS)
    fraction = fraction_index.astype(jnp.float32) / NFRAC
    offset = distance.astype(jnp.float32)
    centre = offset[None, :, :] - (TAPS // 2 - 1) - fraction[:, None, None]
    window_taper = 0.5 - 0.5 * jnp.cos(2.0 * jnp.pi * (offset + 0.5) / TAPS)
    values = jnp.sinc(centre) * window_taper[None, :, :]
    return jnp.where(inside[None, :, :], values, 0.0).astype(jnp.bfloat16)


def filter_rows(source, starts, kernel, sample_count):
    slicer = jax.vmap(
        lambda series, start_at: lax.dynamic_slice_in_dim(
            series, start_at, sample_count + 128, axis=1
        ),
        in_axes=(1, 0),
        out_axes=1,
    )
    pieces = slicer(source, starts)
    row_count = pieces.shape[1]
    blocks = sample_count // 128
    tiles = pieces.reshape(2, row_count, blocks + 1, 128)
    upper = jnp.einsum(
        "crnp,rpv->crnv", tiles[:, :, :blocks], kernel[:, :128], preferred_element_type=jnp.float32
    )
    lower = jnp.einsum(
        "crnp,rpv->crnv", tiles[:, :, 1:], kernel[:, 128:], preferred_element_type=jnp.float32
    )
    return (upper + lower).reshape(2, row_count, sample_count)


def rotate_rows(filtered, phase_rows, rate_rows, slice_length):
    sample_count = filtered.shape[-1]
    position = jnp.arange(sample_count, dtype=jnp.int32).astype(jnp.float32) / slice_length
    cycles = (
        phase_rows.astype(jnp.float32)[:, None] / NPHASE + rate_rows[:, None] * position[None, :]
    )
    phase_angle = 2.0 * jnp.pi * cycles
    cosine = jnp.cos(phase_angle)
    sine_value = jnp.sin(phase_angle)
    real_part = filtered[0] * cosine + filtered[1] * sine_value
    imag_part = filtered[1] * cosine - filtered[0] * sine_value
    return jnp.stack([real_part, imag_part]).astype(jnp.bfloat16)


def rotation_table(indices, radix_size):
    product = indices[:, None] * indices[None, :] % radix_size
    table_angle = product.astype(jnp.float32) * (2.0 * math.pi / radix_size)
    scaling = 1.0 / math.sqrt(radix_size)
    cosine = jnp.cos(table_angle) * scaling
    sine_value = jnp.sin(table_angle) * scaling
    stacked = jnp.stack(
        [jnp.stack([cosine, sine_value], axis=1), jnp.stack([-sine_value, cosine], axis=1)], axis=0
    )
    return stacked.astype(jnp.bfloat16)


def dft_tables():
    along_a = jnp.arange(RADIX_A, dtype=jnp.int32)
    along_b = jnp.arange(RADIX_B, dtype=jnp.int32)
    first_table = rotation_table(along_a, RADIX_A)
    second_table = rotation_table(along_b, RADIX_B)
    product = along_a[:, None] * along_b[None, :] % CHANNELS
    twist_angle = product.astype(jnp.float32) * (2.0 * math.pi / CHANNELS)
    twiddle = jnp.stack([jnp.cos(twist_angle), jnp.sin(twist_angle)])
    return (first_table, twiddle, second_table)


def transform(rotated, tables, block_width):
    first_table, twiddle, second_table = tables
    row_count = rotated.shape[1]
    frames = rotated.shape[2] // CHANNELS
    arranged = rotated.reshape(2, row_count, frames, RADIX_A, RADIX_B)
    section_half = jnp.einsum(
        "pkcn,crfnm->prfkm", first_table, arranged, preferred_element_type=jnp.float32
    )
    real_part = section_half[0] * twiddle[0] + section_half[1] * twiddle[1]
    imag_part = section_half[1] * twiddle[0] - section_half[0] * twiddle[1]
    partial_value = jnp.stack([real_part, imag_part]).astype(jnp.bfloat16)
    block_count = CHANNELS // block_width
    if block_width <= RADIX_A:
        split_rows = partial_value.reshape(
            2, row_count, frames, RADIX_A // block_width, block_width, RADIX_B
        )
        spectrum = jnp.einsum(
            "qjpm,prfakm->rfjaqk", second_table, split_rows, preferred_element_type=jnp.float32
        )
    else:
        split_table = second_table.reshape(2, block_count, block_width // RADIX_A, 2, RADIX_B)
        spectrum = jnp.einsum(
            "qJjpm,prfkm->rfJqjk", split_table, partial_value, preferred_element_type=jnp.float32
        )
    return spectrum.astype(jnp.bfloat16).reshape(row_count, frames, block_count, 2 * block_width)


def correlate(spectra):
    frame_total = spectra.shape[2]
    turned = jnp.stack([-spectra[:, :, :, 1], spectra[:, :, :, 0]], axis=3)
    partner = jnp.concatenate([spectra, turned], axis=1)
    summed = jnp.einsum("bifck,bjfck->bkij", spectra, partner, preferred_element_type=jnp.float32)
    return summed / frame_total


def local_wide(voltages, sample_delay, frac_index, phase_index, fringe_rate):
    band_count = voltages.shape[1]
    station_count = voltages.shape[2]
    length = voltages.shape[3]
    frames = length // CHANNELS
    row_count = band_count * station_count
    flattened = voltages.reshape(2, row_count, length)
    delays = jnp.broadcast_to(sample_delay[:, 0][None, :], (band_count, station_count)).reshape(
        row_count
    )
    kernel = toeplitz_of(frac_index[:, 0])
    kernel_rows = jnp.broadcast_to(kernel[None], (band_count,) + kernel.shape).reshape(
        (row_count,) + kernel.shape[1:]
    )
    phase_rows = phase_index[:, :, 0].reshape(row_count)
    rate_rows = fringe_rate.reshape(row_count)
    rim_width = MAXD + TAPS - 1
    following = shifted(flattened[:, :, :rim_width], "tm", -1)
    padding = jnp.zeros((2, row_count, 129 - TAPS), flattened.dtype)
    source = jnp.concatenate([flattened, following, padding], axis=2)
    rotated = rotate_rows(
        filter_rows(source, delays, kernel_rows, length), phase_rows, rate_rows, length
    )
    slices = lax.axis_size("tm")
    groups = lax.axis_size("sta")
    block_width = CHANNELS // (slices * groups)
    spectra = transform(rotated, dft_tables(), block_width)
    packed = spectra.reshape(band_count, station_count, frames, slices, groups, 2 * block_width)
    received = lax.all_to_all(
        lax.all_to_all(packed, "tm", split_axis=3, concat_axis=2, tiled=True),
        "sta",
        split_axis=4,
        concat_axis=1,
        tiled=True,
    )
    gathered = received.reshape(band_count, station_count * groups, slices * frames, 2, block_width)
    return correlate(gathered)


ROWS = CHANNELS // 128
REACH = MAXD // 128 + 1
STRIDE = ROWS + REACH + 7
WINDOW = 384
ABOVE = 128
TALL = ABOVE + WINDOW
MESH = pl.DeviceIdType.MESH


def delay_filters(frac_index):
    kernel = toeplitz_of(frac_index)[:, : 128 + TAPS].astype(jnp.float32)
    kernel = jnp.pad(kernel, ((0, 0), (ABOVE, TALL - ABOVE - 128 - TAPS), (0, 0)))
    return kernel.reshape(-1, 128)


def phasors(phase_index, fringe_rate, length):
    starts = jnp.arange(length // 128, dtype=jnp.int32).astype(jnp.float32) * 128 / length
    within = jnp.arange(128, dtype=jnp.int32).astype(jnp.float32) / length
    start_angle = 2.0 * jnp.pi * (
        phase_index.astype(jnp.float32)[..., None] / NPHASE + fringe_rate[..., None] * starts
    )
    within_angle = 2.0 * jnp.pi * (fringe_rate[..., None] * within)
    coarse = jnp.stack([jnp.cos(start_angle), jnp.sin(start_angle)], axis=2)
    fine = jnp.stack([jnp.cos(within_angle), jnp.sin(within_angle)], axis=2)
    return coarse, fine


def station_band(
    shifts, read_head, read_tail, filter_ref, read_coarse, read_fine, first_ref, twiddle_ref,
    second_ref, write, stations, blocks, series, gathered
):
    for part in range(2):
        for row in range(ROWS + REACH):
            tile = read_head(part, row) if row < ROWS else read_tail(part, row - ROWS)
            series[part, pl.ds(row, stations, stride=STRIDE), :] = tile.astype(jnp.float32)
        series[part, pl.ds(ROWS + REACH, stations, stride=STRIDE), :] = jnp.zeros(
            (stations, 128), jnp.float32
        )

    def across(row):
        return jnp.transpose(jnp.broadcast_to(row, (128, 128)))

    def one(station):
        base = station * STRIDE + shifts[0, station]
        parts = []
        for part in range(2):
            pieces = [
                series[part, pl.ds(base + step, ROWS), :].astype(jnp.bfloat16) for step in range(3)
            ]
            parts.append(jnp.concatenate(pieces, axis=1))
        taps = filter_ref[pl.ds(station * TALL + ABOVE - shifts[1, station], WINDOW), :]
        filtered = jnp.dot(
            jnp.concatenate(parts, axis=0), taps.astype(jnp.bfloat16),
            preferred_element_type=jnp.float32,
        )
        coarse = read_coarse(station)
        fine = read_fine(station)
        cos_a, sin_a = across(coarse[0:1]), across(coarse[1:2])
        cos_b, sin_b = fine[0:1], fine[1:2]
        cosine = cos_a * cos_b - sin_a * sin_b
        sine = sin_a * cos_b + cos_a * sin_b
        re, im = filtered[:ROWS], filtered[ROWS:]
        return jnp.concatenate(
            [re * cosine + im * sine, im * cosine - re * sine], axis=0
        ).astype(jnp.bfloat16)

    def pair(at, carry):
        rotated = jnp.concatenate([one(2 * at), one(2 * at + 1)], axis=1)
        half = jnp.dot(first_ref[...], rotated, preferred_element_type=jnp.float32)
        cosine, sine = twiddle_ref[0], twiddle_ref[1]
        turned = []
        for which in range(2):
            re = half[:RADIX_A, which * 128 : (which + 1) * 128]
            im = half[RADIX_A:, which * 128 : (which + 1) * 128]
            turned.append(
                jnp.concatenate([re * cosine + im * sine, im * cosine - re * sine], axis=1)
            )
        partial_value = jnp.concatenate(turned, axis=0).astype(jnp.bfloat16)
        spectrum = lax.dot_general(
            second_ref[...], partial_value, (((1,), (1,)), ((), ())),
            preferred_element_type=jnp.float32,
        )
        for which in range(2):
            gathered[pl.ds(2 * at + which, 2 * RADIX_B, stride=stations), :] = spectrum[
                :, which * 128 : (which + 1) * 128
            ]
        return carry

    lax.fori_loop(0, stations // 2, pair, 0)
    inner = 2 * RADIX_B // blocks * stations

    def pack(block, carry):
        rows = pl.ds(pl.multiple_of(block * inner, inner), inner)
        write(block, gathered[rows, :].astype(jnp.bfloat16))
        return carry

    lax.fori_loop(0, blocks, pack, 0)


def columns_of(row):
    return slice(row * 128, (row + 1) * 128)


def station_kernel(
    shifts, head_ref, tail_ref, filter_ref, coarse_ref, fine_ref, first_ref, twiddle_ref,
    second_ref, out_ref, series, gathered
):
    def write(block, value):
        out_ref[0, block] = value

    station_band(
        shifts,
        lambda part, row: head_ref[part, 0, :, columns_of(row)],
        lambda part, row: tail_ref[part, 0, :, columns_of(row)],
        filter_ref,
        lambda station: coarse_ref[0, station],
        lambda station: fine_ref[0, station],
        first_ref, twiddle_ref, second_ref, write,
        head_ref.shape[2], out_ref.shape[1], series, gathered,
    )


def station_scratch(stations):
    return [
        pltpu.VMEM((2, stations * STRIDE, 128), jnp.float32),
        pltpu.VMEM((2 * RADIX_B * stations, 128), jnp.float32),
    ]


def station_spectra(voltages, shifts, tail, filters, coarse, fine, tables, blocks):
    _, bands, stations, _ = voltages.shape
    first, twiddle, second = tables
    inner = 2 * RADIX_B // blocks * stations
    whole = lambda shape: pl.BlockSpec(shape, lambda band, rows: (0,) * len(shape))
    return pl.pallas_call(
        station_kernel,
        out_shape=jax.ShapeDtypeStruct((bands, blocks, inner, 128), jnp.bfloat16),
        grid_spec=pltpu.PrefetchScalarGridSpec(
            num_scalar_prefetch=1,
            grid=(bands,),
            in_specs=[
                pl.BlockSpec((2, 1, stations, CHANNELS), lambda band, rows: (0, band, 0, 0)),
                pl.BlockSpec((2, 1, stations, REACH * 128), lambda band, rows: (0, band, 0, 0)),
                whole(filters.shape),
                pl.BlockSpec((1, stations, 2, 128), lambda band, rows: (band, 0, 0, 0)),
                pl.BlockSpec((1, stations, 2, 128), lambda band, rows: (band, 0, 0, 0)),
                whole(first.shape),
                whole(twiddle.shape),
                whole(second.shape),
            ],
            out_specs=pl.BlockSpec((1, blocks, inner, 128), lambda band, rows: (band, 0, 0, 0)),
            scratch_shapes=station_scratch(stations),
        ),
        compiler_params=pltpu.CompilerParams(vmem_limit_bytes=48 * 2**20),
        cost_estimate=pl.CostEstimate(
            flops=4 * 10**9, bytes_accessed=10 * 2**20, transcendentals=0
        ),
    )(shifts, voltages, tail, filters, coarse, fine, first, twiddle, second)


def stream_kernel(
    shifts, voltages_ref, tail_ref, sent_ref, filter_ref, coarse_ref, fine_ref, first_ref,
    twiddle_ref, second_ref, got_ref, last_ref, heads, tails, ready, series, gathered,
    send_sem, recv_sem, own_sem, load_sem
):
    times, groups = lax.axis_size("tm"), lax.axis_size("sta")
    count = times * groups
    at_time, at_group = lax.axis_index("tm"), lax.axis_index("sta")
    me = at_time * groups + at_group
    bands = sent_ref.shape[0]
    stations = heads.shape[2]
    barrier = pltpu.get_barrier_semaphore()

    def greet(step, carry):
        other = lax.rem(me + step, count)
        pl.semaphore_signal(
            barrier, inc=1, device_id=(other // groups, lax.rem(other, groups)),
            device_id_type=MESH,
        )
        return carry

    load_head = pltpu.make_async_copy(
        voltages_ref.at[:, :, :, pl.ds(CHANNELS, CHANNELS)], heads, load_sem.at[0]
    )
    load_tail = pltpu.make_async_copy(tail_ref, tails, load_sem.at[1])
    load_head.start()
    load_tail.start()
    lax.fori_loop(1, count, greet, 0)
    pl.semaphore_wait(barrier, count - 1)

    def copy_to(other, source, target, chunk):
        return pltpu.make_async_remote_copy(
            src_ref=source,
            dst_ref=target,
            send_sem=send_sem.at[chunk],
            recv_sem=recv_sem.at[chunk],
            device_id=(other // groups, lax.rem(other, groups)),
            device_id_type=MESH,
        )

    def send_all(source, target, band, chunk):
        def send(step, carry):
            other = lax.rem(me + step, count)
            copy_to(other, source.at[band, other], target.at[band, me], chunk).start()
            return carry

        lax.fori_loop(1, count, send, 0)

    def first_frame(band, carry):
        send_all(sent_ref, got_ref, band, band)
        return carry

    lax.fori_loop(0, bands, first_frame, 0)
    own = pltpu.make_async_copy(sent_ref.at[:, me], got_ref.at[:, me], own_sem.at[0])
    own.start()
    load_head.wait()
    load_tail.wait()

    def second_frame(band, carry):
        def write(block, value):
            ready[band, block] = value

        station_band(
            shifts,
            lambda part, row: heads[part, band, :, columns_of(row)],
            lambda part, row: tails[part, band, :, columns_of(row)],
            filter_ref,
            lambda station: coarse_ref[band, station],
            lambda station: fine_ref[band, station],
            first_ref, twiddle_ref, second_ref, write,
            stations, count, series, gathered,
        )
        send_all(ready, last_ref, band, bands + band)
        return carry

    lax.fori_loop(0, bands, second_frame, 0)
    own_last = pltpu.make_async_copy(ready.at[:, me], last_ref.at[:, me], own_sem.at[1])
    own_last.start()
    for chunk in range(2 * bands):
        source, target = (sent_ref, got_ref) if chunk < bands else (ready, last_ref)
        every = pltpu.make_async_remote_copy(
            src_ref=source.at[chunk % bands, pl.ds(0, count - 1)],
            dst_ref=target.at[chunk % bands, pl.ds(0, count - 1)],
            send_sem=send_sem.at[chunk],
            recv_sem=recv_sem.at[chunk],
            device_id=(at_time, at_group),
            device_id_type=MESH,
        )
        every.wait_send()
        every.wait_recv()
    own.wait()
    own_last.wait()


def stream(shifts, voltages, tail, sent, filters, coarse, fine, tables):
    _, bands, stations, _ = voltages.shape
    inside = pl.BlockSpec(memory_space=pltpu.VMEM)
    outside = pl.BlockSpec(memory_space=pl.ANY)
    shape = jax.ShapeDtypeStruct(sent.shape, sent.dtype)
    return pl.pallas_call(
        stream_kernel,
        out_shape=(shape, shape),
        in_specs=[pl.BlockSpec(memory_space=pltpu.SMEM)] + [outside] * 3 + [inside] * 6,
        out_specs=(outside, outside),
        scratch_shapes=[
            pltpu.VMEM((2, bands, stations, CHANNELS), voltages.dtype),
            pltpu.VMEM(tail.shape, tail.dtype),
            pltpu.VMEM(sent.shape, sent.dtype),
        ]
        + station_scratch(stations)
        + [
            pltpu.SemaphoreType.DMA((2 * bands,)),
            pltpu.SemaphoreType.DMA((2 * bands,)),
            pltpu.SemaphoreType.DMA((2,)),
            pltpu.SemaphoreType.DMA((2,)),
        ],
        compiler_params=pltpu.CompilerParams(
            collective_id=0, has_side_effects=True, vmem_limit_bytes=48 * 2**20
        ),
        cost_estimate=pl.CostEstimate(
            flops=4 * 10**9, bytes_accessed=600 * 2**20, transcendentals=0
        ),
    )(shifts, voltages, tail, sent, filters, coarse, fine, *tables)


def correlate_kernel(scale, *refs):
    frame_refs, out_ref, turned = refs[:-2], refs[-2], refs[-1]
    times, groups = frame_refs[0].shape[1], frame_refs[0].shape[2]
    frames = times * len(frame_refs)
    stations = groups * frame_refs[0].shape[5]
    stride = frames + 8
    at = 0
    for ref in frame_refs:
        for time in range(times):
            both = [
                ref[0, time, group, 0, part] for part in range(2) for group in range(groups)
            ]
            turned[pl.ds(at, 128, stride=stride), :] = jnp.transpose(
                jnp.concatenate(both, axis=0).astype(jnp.float32)
            )
            at += 1
    many = 128 // frames
    lane = lax.broadcasted_iota(jnp.int32, (128, 128), 1)
    sign = jnp.where(lane < stations, 1.0, -1.0).astype(jnp.bfloat16)
    owner = lax.broadcasted_iota(jnp.int32, (stations, 256), 1) % 128 // frames

    def step(group, carry):
        block = jnp.concatenate(
            [
                turned[pl.ds(pl.multiple_of((group * many + one) * stride, 8), frames), :]
                for one in range(many)
            ],
            axis=0,
        ).astype(jnp.bfloat16)
        flipped = jnp.transpose(block)
        left = jnp.concatenate([flipped[:stations], flipped[stations:]], axis=1)
        swapped = jnp.concatenate([block[:, stations:], block[:, :stations]], axis=1)
        right = jnp.concatenate([block * sign, swapped], axis=0)
        spread = jnp.concatenate(
            [jnp.where(owner == one, left, jnp.zeros_like(left)) for one in range(many)], axis=0
        )
        result = jnp.dot(spread, right, preferred_element_type=jnp.float32)
        for one in range(many):
            out_ref[0, group * many + one] = result[one * stations : (one + 1) * stations] * scale
        return carry

    lax.fori_loop(0, 128 // many, step, 0, unroll=True)


def correlate_frames(frames, times, groups, stations):
    bands, _, inner, _ = frames[0].shape
    columns = inner // (2 * stations)
    depth = 2 * times * len(frames)
    shaped = [
        frame.reshape(bands, times, groups, columns, 2, stations, 128) for frame in frames
    ]
    total = groups * stations
    return pl.pallas_call(
        functools.partial(correlate_kernel, 2.0 / depth),
        out_shape=jax.ShapeDtypeStruct((bands, columns * 128, total, 2 * total), jnp.float32),
        grid=(bands, columns),
        in_specs=[
            pl.BlockSpec(
                (1, times, groups, 1, 2, stations, 128),
                lambda band, column: (band, 0, 0, column, 0, 0, 0),
            )
            for _ in frames
        ],
        out_specs=pl.BlockSpec(
            (1, 128, total, 2 * total), lambda band, column: (band, column, 0, 0)
        ),
        scratch_shapes=[pltpu.VMEM((128 * (depth // 2 + 8), 128), jnp.float32)],
        compiler_params=pltpu.CompilerParams(vmem_limit_bytes=58 * 2**20),
    )(*shaped)


def flat_tables():
    first, twiddle, second = dft_tables()
    first = first.reshape(2 * RADIX_A, 2 * RADIX_A)
    second = jnp.transpose(second, (1, 0, 2, 3)).reshape(2 * RADIX_B, 2 * RADIX_B)
    return first, twiddle, second


def local_narrow(voltages, sample_delay, frac_index, phase_index, fringe_rate):
    length = voltages.shape[3]
    times, groups = lax.axis_size("tm"), lax.axis_size("sta")
    reach = REACH * 128
    following = shifted(voltages[..., :reach], "tm", -1)
    delay = sample_delay[:, 0]
    shifts = jnp.stack([delay // 128, delay % 128])
    filters = delay_filters(frac_index[:, 0])
    coarse, fine = phasors(phase_index[:, :, 0], fringe_rate, length)
    tables = flat_tables()
    middle = voltages[..., CHANNELS : CHANNELS + reach]
    early, late = coarse[..., :ROWS], coarse[..., ROWS:]
    sent = station_spectra(
        voltages, shifts, middle, filters, early, fine, tables, times * groups
    )
    received = stream(shifts, voltages, following, sent, filters, late, fine, tables)
    return correlate_frames(received, times, groups, voltages.shape[2])


def local(voltages, *others):
    stations = voltages.shape[2] * lax.axis_size("sta")
    block_width = CHANNELS // (lax.axis_size("tm") * lax.axis_size("sta"))
    depth = 2 * lax.axis_size("tm") * (voltages.shape[3] // CHANNELS)
    fits = voltages.shape[2] % 16 == 0 and block_width % 128 == 0 and depth == 32
    if fits and stations == 64 and voltages.shape[3] == 2 * CHANNELS:
        return local_narrow(voltages, *others)
    return local_wide(voltages, *others)


def solution(mesh):
    return jax.shard_map(
        local,
        mesh=mesh,
        in_specs=(
            P(None, None, "sta", "tm"),
            P("sta", "tm"),
            P("sta", "tm"),
            P(None, "sta", "tm"),
            P(None, "sta"),
        ),
        out_specs=P(None, ("tm", "sta"), None, None),
        check_vma=False,
    )
```
